32 devices in a mesh: group: 2 (over x), cell: 8 (over z, y), member: 2 (over core).
Axes of the slice: x: 2, y: 2, z: 4, core: 2. Of those that a mesh axis runs over, the one named last changes fastest.
Arguments:
- log_perm: float32 [16, 256, 16, 128], P('member', ('group', 'cell')), parts along dimension 1, may hold values from -4 to 4
- pressure: float32 [16, 256, 16, 128], P('member', ('group', 'cell')), parts along dimension 1, may hold values from -6 to 6
- saturation: float32 [16, 256, 16, 128], P('member', ('group', 'cell')), parts along dimension 1, may hold values from 0.1 to 0.9
- storage: float32 [256, 16, 128], P(('group', 'cell')), parts along dimension 0, may hold values from 0.05 to 0.5
- source: float32 [256, 16, 128], P(('group', 'cell')), parts along dimension 0, may hold values from -6 to 6
- active: int32 [256, 16, 128], P(('group', 'cell')), parts along dimension 0, may hold values 0 or 1
- wells: int32 [128], P('group'), parts along dimension 0, may hold values from 0 to 262143
- observed: float32 [256], P('group'), parts along dimension 0, may hold values from -6 to 6
- observation_variance: float32 [256], P('group'), parts along dimension 0, may hold values from 0.05 to 0.5
- noise: float32 [32, 128], P('group'), parts along dimension 0, may hold values from -5 to 5
Outputs:
- updated_perm: float32 [16, 256, 16, 128], P('member', ('group', 'cell')), parts along dimension 1
- pressure_out: float32 [16, 256, 16, 128], P('member', ('group', 'cell')), parts along dimension 1
- saturation_out: float32 [16, 256, 16, 128], P('member', ('group', 'cell')), parts along dimension 1
- predicted: float32 [32, 128], P(('group', 'member')), parts along dimension 0
The draws below stay inside these ranges and needn't reach their ends.
There are 2 independent parts, one for each index of `group`. The reference program is written for one: setup_inputs(seed, part) draws one part's arguments, and reference() takes and returns one part's arrays. A program takes and returns all parts, laid end to end along the dimension named above; each array names one. Nothing has to cross between parts.
All inputs are finite; a program needn't handle non-finite values. No bound on the sum of `active` on one device may be relied on, other than what follows from the above.
Results may differ from the reference program's by a relative error of at most 0.0003.
Values sent between devices are 32-bit elements; how exact they have to be, the bound alone decides.
A program may use at most 128 MiB of HBM per device.

```python
import math
import jax
import jax.numpy as jnp
from jax import lax

CY = 16
CZ = 128
ITERS = 3
NW = 64
ND = 128
MEMBERS = 16
NX = 128


def place_ends(entries, rng, smallest, high):
    longest = entries.shape.index(max(entries.shape))
    spots = []
    for shift in (0, 1):
        where = [jax.random.randint(jax.random.fold_in(rng, axis), (), 0, length) for axis, length in enumerate(entries.shape)]
        where[longest] = (where[longest] + shift) % entries.shape[longest]
        spots.append(tuple(where))
    return entries.at[spots[0]].set(smallest).at[spots[1]].set(high)


def levels(rng, dims, shards, smallest, high):
    gain = 1.0
    for axis_at, blocks in shards:
        steps = jax.random.uniform(jax.random.fold_in(jax.random.fold_in(rng, 6), axis_at), (blocks,), jnp.float32, smallest / len(shards), high / len(shards))
        gain = gain * jnp.repeat(jnp.exp(steps), dims[axis_at] // blocks).reshape((-1,) + (1,) * (len(dims) - 1 - axis_at))
    return gain


def scatter_about(rng, shape, scale, bound, pieces=(), kind=jnp.bfloat16):
    values = scale * jax.random.normal(rng, shape, jnp.float32)
    if pieces:
        values = values * levels(rng, shape, pieces, -0.22, 0.18)
    return jnp.clip(values, -bound, bound).astype(kind)


def setup_inputs(seed: int = 0, part: int = 0) -> dict:
    splits = jax.random.split(jax.random.key(seed), 11)
    own_keys = jax.random.split(jax.random.fold_in(splits[10], part), 11)
    return {
        "log_perm": scatter_about(own_keys[0], (MEMBERS, NX, CY, CZ), 1.0, 4.0, ((0, 2), (1, 8)), jnp.float32),
        "pressure": scatter_about(own_keys[1], (MEMBERS, NX, CY, CZ), 1.0, 6.0, ((0, 2), (1, 8)), jnp.float32),
        "saturation": jnp.clip(0.1 + 0.79999997 * jax.random.uniform(own_keys[2], (MEMBERS, NX, CY, CZ), jnp.float32) ** levels(own_keys[2], (MEMBERS, NX, CY, CZ), ((0, 2), (1, 8)), -0.2, 0.2), 0.1, 0.9),
        "storage": jnp.clip(jnp.exp(math.log(0.5) - 2.3025851 * jax.random.uniform(own_keys[3], (NX, CY, CZ), jnp.float32) ** levels(own_keys[3], (NX, CY, CZ), ((0, 8),), -0.2, 0.2)), 0.05, 0.5),
        "source": scatter_about(own_keys[4], (NX, CY, CZ), 1.0, 6.0, ((0, 8),), jnp.float32),
        "active": place_ends((jax.random.randint(own_keys[5], (NX, CY, CZ), 0, 8) < 7).astype(jnp.int32), jax.random.fold_in(own_keys[5], 1), 0, 1),
        "wells": place_ends(jax.random.randint(own_keys[6], (NW,), 0, NX * CY * CZ), jax.random.fold_in(own_keys[6], 1), 0, (NX * CY * CZ) - 1).astype(jnp.int32),
        "observed": scatter_about(own_keys[7], (ND,), 1.0, 6.0, (), jnp.float32),
        "observation_variance": jnp.clip(jnp.exp(jax.random.uniform(own_keys[8], (ND,), jnp.float32, math.log(0.05), math.log(0.5))), 0.05, 0.5),
        "noise": scatter_about(own_keys[9], (MEMBERS, ND), 1.0, 5.0, (), jnp.float32),
    }


INFLATION_FACTOR = 4.0
TIME_STEP = 0.02

def pad_all(values):
    return jnp.pad(values, ((0, 0), (1, 1), (1, 1), (1, 1)))

def neighbours(padded_field):
    return [padded_field[..., 2:, 1:-1, 1:-1], padded_field[..., :-2, 1:-1, 1:-1], padded_field[..., 1:-1, 2:, 1:-1], padded_field[..., 1:-1, :-2, 1:-1], padded_field[..., 1:-1, 1:-1, 2:], padded_field[..., 1:-1, 1:-1, :-2]]

def reference(log_perm, pressure, saturation, storage, source, active, wells, observed, observation_variance, noise):
    members = log_perm.shape[0]
    scaled = active.astype(jnp.float32)[None] * jnp.exp(0.5 * log_perm)
    conduct = [scaled * other for other in neighbours(pad_all(scaled))]
    balance = storage[None] + sum(conduct)
    rhs = storage[None] * pressure + source[None]
    pres_field = pressure
    for step in range(ITERS):
        inflow = sum((link * other for link, other in zip(conduct, neighbours(pad_all(pres_field)))))
        pres_field = (rhs + inflow) / balance
    near_pres = neighbours(pad_all(pres_field))
    near_sat = neighbours(pad_all(saturation))
    change = jnp.zeros_like(saturation)
    for link, pres_near, sat_near in zip(conduct, near_pres, near_sat):
        flux_value = link * (pres_near - pres_field)
        upwind_choice = jnp.where(flux_value > 0, sat_near, saturation)
        change = change + flux_value * upwind_choice * upwind_choice
    sat_new = saturation + TIME_STEP * change / storage[None]
    flat_pres = pres_field.reshape(members, -1)
    flat_sat = sat_new.reshape(members, -1)
    predicted = jnp.concatenate([jnp.take(flat_pres, wells, axis=1), jnp.take(flat_sat, wells, axis=1)], axis=1)
    centre = lax.optimization_barrier(jnp.mean(predicted, axis=0))
    member_deviation = (predicted - centre[None]) / jnp.sqrt(jnp.float32(members - 1))
    covariance_matrix = jnp.dot(member_deviation.T, member_deviation, precision=lax.Precision.HIGHEST) + INFLATION_FACTOR * jnp.diag(observation_variance)
    data_mismatch = observed[None] + jnp.sqrt(INFLATION_FACTOR * observation_variance)[None] * noise - predicted
    factor = jnp.linalg.cholesky(covariance_matrix)
    solved = jax.scipy.linalg.cho_solve((factor, True), data_mismatch.T)
    weights = jnp.dot(member_deviation, solved, precision=lax.Precision.HIGHEST)
    flat_perm = log_perm.reshape(members, -1)
    mixed = jnp.dot(weights.T, flat_perm, precision=lax.Precision.HIGHEST)
    updated_perm = log_perm + (mixed / jnp.sqrt(jnp.float32(members - 1))).reshape(log_perm.shape)
    return (updated_perm, pres_field, sat_new, predicted)
```

```python
import functools
import jax
import jax.numpy as jnp
from jax import lax
from jax.experimental import pallas as pl
from jax.experimental.pallas import tpu as pltpu
from jax.sharding import PartitionSpec as P

ITERS = 3
INFLATION_FACTOR = 4.0
TIME_STEP = 0.02
MESH = pl.DeviceIdType.MESH
LP, PR, SAT, Q1, Q2, P3 = range(6)


def kernel(
    ncell,
    lp_hbm, pr_hbm, sat_hbm, sto_hbm, src_hbm, act_hbm, wells, obs, var, noise,
    upd_out, pr_out, sat_out, pred_out,
    lp, lp_peer, pr, sat, sto, src, act,
    s, qa, qb, rhs, rbal, p3, snew, upd,
    halo, act_halo, s_halo, q0_halo, found, wcol,
    load_sems, out_sems, send_sems, recv_sems, act_send, act_recv,
    peer_send, peer_recv, found_send, found_recv,
):
    md, nx, cy, cz = lp.shape
    cell = lax.axis_index("cell")
    mem = lax.axis_index("member")
    other = 1 - mem
    has_left = cell > 0
    has_right = cell < ncell - 1
    left = jnp.maximum(cell - 1, 0)
    right = jnp.minimum(cell + 1, ncell - 1)

    loads = [
        pltpu.make_async_copy(a, b, load_sems.at[i])
        for i, (a, b) in enumerate(
            [(act_hbm, act), (lp_hbm, lp), (pr_hbm, pr), (sto_hbm, sto), (src_hbm, src), (sat_hbm, sat)]
        )
    ]
    for c in loads:
        c.start()

    barrier = pltpu.get_barrier_semaphore()

    def greet(k, carry):
        to = lax.rem(cell + k, ncell)
        pl.semaphore_signal(barrier, inc=1, device_id={"cell": to, "member": other}, device_id_type=MESH)

        @pl.when(k > 0)
        def _():
            pl.semaphore_signal(barrier, inc=1, device_id={"cell": to, "member": mem}, device_id_type=MESH)

        return carry

    lax.fori_loop(0, ncell, greet, 0)
    pl.semaphore_wait(barrier, 2 * ncell - 1)

    def remote(source, dest, ssem, rsem, to):
        return pltpu.make_async_remote_copy(
            src_ref=source, dst_ref=dest, send_sem=ssem, recv_sem=rsem,
            device_id={"cell": to}, device_id_type=MESH,
        )

    def edge_copy(f, side, ref):
        x = nx - 1 if side == 0 else 0
        to = right if side == 0 else left
        return remote(ref.at[:, x], halo.at[f, side], send_sems.at[f, side], recv_sems.at[f, side], to)

    def act_copy(side):
        x = nx - 1 if side == 0 else 0
        to = right if side == 0 else left
        return remote(act_hbm.at[x], act_halo.at[side], act_send.at[side], act_recv.at[side], to)

    def send_edges(f, ref):
        @pl.when(has_left)
        def _():
            edge_copy(f, 1, ref).start()

        @pl.when(has_right)
        def _():
            edge_copy(f, 0, ref).start()

    def wait_edges(f, ref):
        @pl.when(has_left)
        def _():
            edge_copy(f, 0, ref).wait_recv()

        @pl.when(has_right)
        def _():
            edge_copy(f, 1, ref).wait_recv()

    def sent_edges(f, ref):
        @pl.when(has_left)
        def _():
            edge_copy(f, 1, ref).wait_send()

        @pl.when(has_right)
        def _():
            edge_copy(f, 0, ref).wait_send()

    @pl.when(has_left)
    def _():
        act_copy(1).start()

    @pl.when(has_right)
    def _():
        act_copy(0).start()

    send_edges(LP, lp_hbm)
    send_edges(PR, pr_hbm)
    send_edges(SAT, sat_hbm)
    peer = pltpu.make_async_remote_copy(
        src_ref=lp_hbm, dst_ref=lp_peer, send_sem=peer_send, recv_sem=peer_recv,
        device_id={"member": other}, device_id_type=MESH,
    )
    peer.start()

    @pl.when(jnp.logical_not(has_left))
    def _():
        for f in range(6):
            halo[f, 0] = jnp.zeros((md, cy, cz), jnp.float32)
        s_halo[0] = jnp.zeros((md, cy, cz), jnp.float32)

    @pl.when(jnp.logical_not(has_right))
    def _():
        for f in range(6):
            halo[f, 1] = jnp.zeros((md, cy, cz), jnp.float32)
        s_halo[1] = jnp.zeros((md, cy, cz), jnp.float32)

    lane = lax.broadcasted_iota(jnp.int32, (1, cy, cz), 2)
    row = lax.broadcasted_iota(jnp.int32, (1, cy, cz), 1)

    def z_up(v):
        return pltpu.roll(v, cz - 1, 2)

    def z_down(v):
        return pltpu.roll(v, 1, 2)

    def y_up(v):
        return pltpu.roll(v, cy - 1, 1)

    def y_down(v):
        return pltpu.roll(v, 1, 1)

    def plane_sum(q):
        return (
            jnp.where(lane == cz - 1, 0.0, z_up(q))
            + jnp.where(lane == 0, 0.0, z_down(q))
            + jnp.where(row == cy - 1, 0.0, y_up(q))
            + jnp.where(row == 0, 0.0, y_down(q))
        )

    loads[0].wait()
    loads[1].wait()
    for i in (2, 3, 4):
        loads[i].wait()

    def prepare(x, carry):
        sc = act[x].astype(jnp.float32)[None] * jnp.exp(0.5 * lp[:, x])
        s[:, x] = sc
        pc = pr[:, x]
        qa[:, x] = sc * pc
        rhs[:, x] = sto[x][None] * pc + src[x][None]
        return carry

    lax.fori_loop(0, nx, prepare, 0)

    def balance_at(x, below, above):
        sc = s[:, x]
        total = sto[x][None] + sc * (below + above + plane_sum(sc))
        rbal[:, x] = 1.0 / total

    def sweep_at(x, below, above, old, new, last):
        sc = s[:, x]
        p = (rhs[:, x] + sc * (below + above + plane_sum(old[:, x]))) * rbal[:, x]
        new[:, x] = p if last else sc * p

    def interior(f):
        def step(x, carry):
            f(x)
            return carry

        lax.fori_loop(1, nx - 1, step, 0)

    def first_inside(x):
        balance_at(x, s[:, x - 1], s[:, x + 1])
        sweep_at(x, qa[:, x - 1], qa[:, x + 1], qa, qb, False)

    interior(first_inside)

    for side, there in ((0, has_left), (1, has_right)):
        @pl.when(there)
        def _(side=side):
            act_copy(side).wait_recv()
            edge_copy(LP, side, lp_hbm).wait_recv()
            edge_copy(PR, side, pr_hbm).wait_recv()
            s_halo[side] = act_halo[side].astype(jnp.float32)[None] * jnp.exp(0.5 * halo[LP, side])

        q0_halo[side] = s_halo[side] * halo[PR, side]

    end = nx - 1
    balance_at(0, s_halo[0], s[:, 1])
    sweep_at(0, q0_halo[0], qa[:, 1], qa, qb, False)
    balance_at(end, s[:, end - 1], s_halo[1])
    sweep_at(end, qa[:, end - 1], q0_halo[1], qa, qb, False)
    send_edges(Q1, qb)

    interior(lambda x: sweep_at(x, qb[:, x - 1], qb[:, x + 1], qb, qa, False))
    wait_edges(Q1, qb)
    sweep_at(0, halo[Q1, 0], qb[:, 1], qb, qa, False)
    sweep_at(end, qb[:, end - 1], halo[Q1, 1], qb, qa, False)
    send_edges(Q2, qa)

    interior(lambda x: sweep_at(x, qa[:, x - 1], qa[:, x + 1], qa, p3, True))
    wait_edges(Q2, qa)
    sweep_at(0, halo[Q2, 0], qa[:, 1], qa, p3, True)
    sweep_at(end, qa[:, end - 1], halo[Q2, 1], qa, p3, True)
    send_edges(P3, p3)
    put_p = pltpu.make_async_copy(p3, pr_out, out_sems.at[0])
    put_p.start()
    loads[5].wait()

    def face(sn, pn, tn, pc, tc):
        d = pn - pc
        return sn * (d * jnp.where(d > 0, tn, tc))

    def saturate_at(x, below, above):
        sc = s[:, x]
        pc = p3[:, x]
        raw = sat[:, x]
        tc = raw * raw
        bs, bp, bt = below
        as_, ap, at = above
        change = face(bs, bp, bt * bt, pc, tc) + face(as_, ap, at * at, pc, tc)
        gz = sc * face(jnp.where(lane == cz - 1, 0.0, z_up(sc)), z_up(pc), z_up(tc), pc, tc)
        gy = sc * face(jnp.where(row == cy - 1, 0.0, y_up(sc)), y_up(pc), y_up(tc), pc, tc)
        change = sc * change + (gz - z_down(gz)) + (gy - y_down(gy))
        snew[:, x] = raw + change * (TIME_STEP / sto[x])[None]

    def at_x(x):
        return s[:, x], p3[:, x], sat[:, x]

    interior(lambda x: saturate_at(x, at_x(x - 1), at_x(x + 1)))

    nw = wells.shape[0]
    cells_dev = nx * cy * cz
    col = lax.broadcasted_iota(jnp.int32, (md, 2 * nw), 1)
    p3_rows = p3.reshape(md * nx * cy, cz)
    sn_rows = snew.reshape(md * nx * cy, cz)

    def gather(rows, first):
        def one(w, acc):
            at = wells[w] - cell * cells_dev
            inside = jnp.logical_and(at >= 0, at < cells_dev)
            at = jnp.clip(at, 0, cells_dev - 1)
            line = at // cz
            z = at - line * cz
            v = rows[pl.ds(line, md, stride=nx * cy), :]
            v = pltpu.roll(v, lax.rem(first + w - z + cz, cz), 1)
            keep = jnp.where(inside, w + first, -1)
            return jnp.where(col == keep, v, acc)

        return one

    acc = lax.fori_loop(0, nw, gather(p3_rows, 0), jnp.zeros((md, 2 * nw), jnp.float32), unroll=8)

    wait_edges(SAT, sat_hbm)
    wait_edges(P3, p3)
    saturate_at(0, (s_halo[0], halo[P3, 0], halo[SAT, 0]), at_x(1))
    saturate_at(end, at_x(end - 1), (s_halo[1], halo[P3, 1], halo[SAT, 1]))
    put_s = pltpu.make_async_copy(snew, sat_out, out_sems.at[1])
    put_s.start()
    acc = lax.fori_loop(0, nw, gather(sn_rows, nw), acc, unroll=8)
    found[0, 0] = acc

    def found_copy(k, m):
        return pltpu.make_async_remote_copy(
            src_ref=found.at[0, 0], dst_ref=found.at[m, k],
            send_sem=found_send.at[m, k], recv_sem=found_recv.at[m, k],
            device_id={"cell": lax.rem(cell + k, ncell), "member": mem if m == 0 else other},
            device_id_type=MESH,
        )

    def each_found(act_on):
        def step(k, carry):
            act_on(found_copy(k, 1))

            @pl.when(k > 0)
            def _():
                act_on(found_copy(k, 0))

            return carry

        lax.fori_loop(0, ncell, step, 0)

    each_found(lambda c: c.start())
    each_found(lambda c: c.wait_recv())

    own = found[0, 0]
    far = found[1, 0]
    for k in range(1, ncell):
        own = own + found[0, k]
        far = far + found[1, k]
    pred_out[...] = own

    members = 2 * md
    nd = 2 * nw
    root = float(members - 1) ** 0.5
    both = jnp.concatenate([own, far], axis=0)
    spread = (both - jnp.mean(both, axis=0, keepdims=True)) * (1.0 / root)
    dvar = INFLATION_FACTOR * var[...]
    first = pl.multiple_of(mem * md, md)
    misfit = obs[...] + jnp.sqrt(dvar) * noise[pl.ds(first, md), :] - own
    stack = jnp.concatenate([spread, misfit, jnp.zeros((nd - 3 * md, nd), jnp.float32)], axis=0)
    aug = lax.dot_general(
        spread / dvar, stack, (((1,), (1,)), ((), ())),
        precision=lax.Precision.HIGHEST, preferred_element_type=jnp.float32,
    )
    rid = lax.broadcasted_iota(jnp.int32, (members, nd), 0)
    cid = lax.broadcasted_iota(jnp.int32, (members, nd), 1)
    aug = aug + jnp.where(rid == cid, 1.0, 0.0)
    for k in range(members):
        line = aug[k : k + 1, :] / aug[k : k + 1, k : k + 1]
        aug = jnp.where(rid == k, line, aug - aug[:, k : k + 1] * line)
    for j in range(md):
        wcol[j] = jnp.broadcast_to(aug[:, members + j : members + j + 1] * (1.0 / root), (members, cz))

    peer.wait_recv()
    parts = 4
    share = nx // parts

    def put_u(i):
        return pltpu.make_async_copy(
            upd.at[:, pl.ds(i * share, share)], upd_out.at[:, pl.ds(i * share, share)], out_sems.at[2 + i]
        )

    def mix(x, carry):
        fields = [lp[i, x] for i in range(md)] + [lp_peer[i, x] for i in range(md)]
        for j in range(md):
            total = fields[j]
            for i in range(members):
                total = total + wcol[j, i : i + 1, :] * fields[i]
            upd[j, x] = total
        return carry

    for i in range(parts):
        lax.fori_loop(i * share, (i + 1) * share, mix, 0)
        put_u(i).start()

    each_found(lambda c: c.wait_send())
    peer.wait_send()
    for f, ref in ((LP, lp_hbm), (PR, pr_hbm), (SAT, sat_hbm), (Q1, qb), (Q2, qa), (P3, p3)):
        sent_edges(f, ref)

    @pl.when(has_left)
    def _():
        act_copy(1).wait_send()

    @pl.when(has_right)
    def _():
        act_copy(0).wait_send()

    put_p.wait()
    put_s.wait()
    for i in range(parts):
        put_u(i).wait()


def local(
    log_perm, pressure, saturation, storage, source, active, wells, observed, observation_variance, noise,
):
    md, nx, cy, cz = log_perm.shape
    ncell = lax.axis_size("cell")
    nd = observed.shape[0]
    field = (md, nx, cy, cz)
    plane = (nx, cy, cz)
    f32 = jnp.float32
    any_spec = pl.BlockSpec(memory_space=pl.ANY)
    vmem_spec = pl.BlockSpec(memory_space=pltpu.VMEM)
    dma = pltpu.SemaphoreType.DMA
    return pl.pallas_call(
        functools.partial(kernel, ncell),
        out_shape=[jax.ShapeDtypeStruct(field, f32)] * 3 + [jax.ShapeDtypeStruct((md, nd), f32)],
        in_specs=[any_spec] * 6 + [pl.BlockSpec(memory_space=pltpu.SMEM)] + [vmem_spec] * 3,
        out_specs=[any_spec] * 3 + [vmem_spec],
        scratch_shapes=[
            pltpu.VMEM(field, f32), pltpu.VMEM(field, f32), pltpu.VMEM(field, f32), pltpu.VMEM(field, f32),
            pltpu.VMEM(plane, f32), pltpu.VMEM(plane, f32), pltpu.VMEM(plane, jnp.int32),
            *[pltpu.VMEM(field, f32) for _ in range(8)],
            pltpu.VMEM((6, 2, md, cy, cz), f32),
            pltpu.VMEM((2, cy, cz), jnp.int32),
            pltpu.VMEM((2, md, cy, cz), f32),
            pltpu.VMEM((2, md, cy, cz), f32),
            pltpu.VMEM((2, ncell, md, nd), f32),
            pltpu.VMEM((md, 2 * md, cz), f32),
            dma((6,)), dma((6,)), dma((6, 2)), dma((6, 2)), dma((2,)), dma((2,)),
            dma, dma, dma((2, ncell)), dma((2, ncell)),
        ],
        compiler_params=pltpu.CompilerParams(
            collective_id=0, has_side_effects=True, vmem_limit_bytes=58 * 1024 * 1024
        ),
    )(
        log_perm, pressure, saturation, storage, source, active, wells,
        observed.reshape(1, nd), observation_variance.reshape(1, nd), noise,
    )


def solution(mesh):
    block = P("member", ("group", "cell"), None, None)
    shared = P(("group", "cell"), None, None)
    in_specs = (block, block, block, shared, shared, shared, P("group"), P("group"), P("group"), P("group", None))
    out_specs = (block, block, block, P(("group", "member"), None))
    return jax.shard_map(local, mesh=mesh, in_specs=in_specs, out_specs=out_specs, check_vma=False)
```

```python
import functools
import jax
import jax.numpy as jnp
from jax import lax
from jax.experimental import pallas as pl
from jax.experimental.pallas import tpu as pltpu
from jax.sharding import PartitionSpec as P

ITERS = 3
INFLATION_FACTOR = 4.0
TIME_STEP = 0.02
MESH = pl.DeviceIdType.MESH
LP, PR, SAT, Q1, Q2, P3 = range(6)
HALVES = 2


def kernel(
    ncell,
    lp_hbm, pr_hbm, sat_hbm, sto_hbm, src_hbm, act_hbm, wells,
    lp, lp_peer, p3, snew, own_out, far_out,
    pr, sat, sto, src, act,
    s, qa, qb, rhs, rbal,
    halo, act_halo, s_halo, q0_halo, found,
    load_sems, send_sems, recv_sems, act_send, act_recv,
    peer_send, peer_recv, found_send, found_recv,
):
    md, nx, cy, cz = lp.shape
    cell = lax.axis_index("cell")
    mem = lax.axis_index("member")
    other = 1 - mem
    has_left = cell > 0
    has_right = cell < ncell - 1
    left = jnp.maximum(cell - 1, 0)
    right = jnp.minimum(cell + 1, ncell - 1)

    loads = [
        pltpu.make_async_copy(a, b, load_sems.at[i])
        for i, (a, b) in enumerate(
            [(act_hbm, act), (lp_hbm, lp), (pr_hbm, pr), (sto_hbm, sto), (src_hbm, src), (sat_hbm, sat)]
        )
    ]
    for c in loads:
        c.start()

    barrier = pltpu.get_barrier_semaphore()

    def greet(k, carry):
        to = lax.rem(cell + k, ncell)
        pl.semaphore_signal(barrier, inc=1, device_id={"cell": to, "member": other}, device_id_type=MESH)

        @pl.when(k > 0)
        def _():
            pl.semaphore_signal(barrier, inc=1, device_id={"cell": to, "member": mem}, device_id_type=MESH)

        return carry

    lax.fori_loop(0, ncell, greet, 0)
    pl.semaphore_wait(barrier, 2 * ncell - 1)

    def remote(source, dest, ssem, rsem, to):
        return pltpu.make_async_remote_copy(
            src_ref=source, dst_ref=dest, send_sem=ssem, recv_sem=rsem,
            device_id={"cell": to}, device_id_type=MESH,
        )

    half = md // HALVES
    groups = [pl.ds(g * half, half) for g in range(HALVES)]

    def edge_copy(f, side, ref, g):
        x = nx - 1 if side == 0 else 0
        to = right if side == 0 else left
        part = groups[g]
        return remote(
            ref.at[part, x], halo.at[f, side, part], send_sems.at[f, side, g], recv_sems.at[f, side, g], to
        )

    def act_copy(side):
        x = nx - 1 if side == 0 else 0
        to = right if side == 0 else left
        return remote(act_hbm.at[x], act_halo.at[side], act_send.at[side], act_recv.at[side], to)

    def send_edges(f, ref, g):
        @pl.when(has_left)
        def _():
            edge_copy(f, 1, ref, g).start()

        @pl.when(has_right)
        def _():
            edge_copy(f, 0, ref, g).start()

    def wait_edges(f, ref, g):
        @pl.when(has_left)
        def _():
            edge_copy(f, 0, ref, g).wait_recv()

        @pl.when(has_right)
        def _():
            edge_copy(f, 1, ref, g).wait_recv()

    def sent_edges(f, ref, g):
        @pl.when(has_left)
        def _():
            edge_copy(f, 1, ref, g).wait_send()

        @pl.when(has_right)
        def _():
            edge_copy(f, 0, ref, g).wait_send()

    @pl.when(has_left)
    def _():
        act_copy(1).start()

    @pl.when(has_right)
    def _():
        act_copy(0).start()

    for g in range(HALVES):
        send_edges(LP, lp_hbm, g)
        send_edges(PR, pr_hbm, g)
    for g in range(HALVES):
        send_edges(SAT, sat_hbm, g)
    peer = pltpu.make_async_remote_copy(
        src_ref=lp_hbm, dst_ref=lp_peer, send_sem=peer_send, recv_sem=peer_recv,
        device_id={"member": other}, device_id_type=MESH,
    )
    peer.start()

    @pl.when(jnp.logical_not(has_left))
    def _():
        for f in range(6):
            halo[f, 0] = jnp.zeros((md, cy, cz), jnp.float32)
        s_halo[0] = jnp.zeros((md, cy, cz), jnp.float32)

    @pl.when(jnp.logical_not(has_right))
    def _():
        for f in range(6):
            halo[f, 1] = jnp.zeros((md, cy, cz), jnp.float32)
        s_halo[1] = jnp.zeros((md, cy, cz), jnp.float32)

    lane = lax.broadcasted_iota(jnp.int32, (1, cy, cz), 2)
    row = lax.broadcasted_iota(jnp.int32, (1, cy, cz), 1)

    def z_up(v):
        return pltpu.roll(v, cz - 1, 2)

    def z_down(v):
        return pltpu.roll(v, 1, 2)

    def y_up(v):
        return pltpu.roll(v, cy - 1, 1)

    def y_down(v):
        return pltpu.roll(v, 1, 1)

    def plane_sum(q):
        return (
            jnp.where(lane == cz - 1, 0.0, z_up(q))
            + jnp.where(lane == 0, 0.0, z_down(q))
            + jnp.where(row == cy - 1, 0.0, y_up(q))
            + jnp.where(row == 0, 0.0, y_down(q))
        )

    loads[0].wait()
    loads[1].wait()
    for i in (2, 3, 4):
        loads[i].wait()

    def prepare(x, carry):
        sc = act[x].astype(jnp.float32)[None] * jnp.exp(0.5 * lp[:, x])
        s[:, x] = sc
        pc = pr[:, x]
        qa[:, x] = sc * pc
        rhs[:, x] = sto[x][None] * pc + src[x][None]
        return carry

    lax.fori_loop(0, nx, prepare, 0)

    def balance_at(m, x, below, above):
        sc = s[m, x]
        total = sto[x][None] + sc * (below + above + plane_sum(sc))
        rbal[m, x] = 1.0 / total

    def sweep_at(m, x, below, above, old, new, last):
        sc = s[m, x]
        p = (rhs[m, x] + sc * (below + above + plane_sum(old[m, x]))) * rbal[m, x]
        new[m, x] = p if last else sc * p

    inner = nx - 2
    width = max(d for d in range(1, 8) if inner % d == 0)

    def interior(f):
        def step(i, carry):
            for j in range(width):
                f(1 + i * width + j)
            return carry

        lax.fori_loop(0, inner // width, step, 0)

    end = nx - 1

    def first_inside(m):
        def f(x):
            balance_at(m, x, s[m, x - 1], s[m, x + 1])
            sweep_at(m, x, qa[m, x - 1], qa[m, x + 1], qa, qb, False)

        interior(f)

    for m in groups:
        first_inside(m)

    for g, m in enumerate(groups):
        for side, there in ((0, has_left), (1, has_right)):
            @pl.when(there)
            def _(side=side, g=g, m=m):
                if g == 0:
                    act_copy(side).wait_recv()
                edge_copy(LP, side, lp_hbm, g).wait_recv()
                edge_copy(PR, side, pr_hbm, g).wait_recv()
                s_halo[side, m] = act_halo[side].astype(jnp.float32)[None] * jnp.exp(0.5 * halo[LP, side, m])

            q0_halo[side, m] = s_halo[side, m] * halo[PR, side, m]
        balance_at(m, 0, s_halo[0, m], s[m, 1])
        sweep_at(m, 0, q0_halo[0, m], qa[m, 1], qa, qb, False)
        balance_at(m, end, s[m, end - 1], s_halo[1, m])
        sweep_at(m, end, qa[m, end - 1], q0_halo[1, m], qa, qb, False)
        send_edges(Q1, qb, g)

    for f, old, new, nf, last in ((Q1, qb, qa, Q2, False), (Q2, qa, p3, P3, True)):
        for g, m in enumerate(groups):
            interior(lambda x: sweep_at(m, x, old[m, x - 1], old[m, x + 1], old, new, last))
            wait_edges(f, old, g)
            sweep_at(m, 0, halo[f, 0, m], old[m, 1], old, new, last)
            sweep_at(m, end, old[m, end - 1], halo[f, 1, m], old, new, last)
            send_edges(nf, new, g)
    loads[5].wait()

    def face(sn, pn, tn, pc, tc):
        d = pn - pc
        return sn * (d * jnp.where(d > 0, tn, tc))

    def saturate_at(m, x, below, above):
        sc = s[m, x]
        pc = p3[m, x]
        raw = sat[m, x]
        tc = raw * raw
        bs, bp, bt = below
        as_, ap, at = above
        change = face(bs, bp, bt * bt, pc, tc) + face(as_, ap, at * at, pc, tc)
        gz = sc * face(jnp.where(lane == cz - 1, 0.0, z_up(sc)), z_up(pc), z_up(tc), pc, tc)
        gy = sc * face(jnp.where(row == cy - 1, 0.0, y_up(sc)), y_up(pc), y_up(tc), pc, tc)
        change = sc * change + (gz - z_down(gz)) + (gy - y_down(gy))
        snew[m, x] = raw + change * (TIME_STEP / sto[x])[None]

    def at_x(m, x):
        return s[m, x], p3[m, x], sat[m, x]

    for m in groups:
        interior(lambda x: saturate_at(m, x, at_x(m, x - 1), at_x(m, x + 1)))

    nw = wells.shape[0]
    cells_dev = nx * cy * cz
    col = lax.broadcasted_iota(jnp.int32, (md, 2 * nw), 1)
    p3_rows = p3.reshape(md * nx * cy, cz)
    sn_rows = snew.reshape(md * nx * cy, cz)

    def gather(rows, first):
        def one(w, acc):
            at = wells[w] - cell * cells_dev
            inside = jnp.logical_and(at >= 0, at < cells_dev)
            at = jnp.clip(at, 0, cells_dev - 1)
            line = at // cz
            z = at - line * cz
            v = rows[pl.ds(line, md, stride=nx * cy), :]
            v = pltpu.roll(v, lax.rem(first + w - z + cz, cz), 1)
            keep = jnp.where(inside, w + first, -1)
            return jnp.where(col == keep, v, acc)

        return one

    acc = lax.fori_loop(0, nw, gather(p3_rows, 0), jnp.zeros((md, 2 * nw), jnp.float32), unroll=8)

    for g, m in enumerate(groups):
        wait_edges(SAT, sat_hbm, g)
        wait_edges(P3, p3, g)
        saturate_at(m, 0, (s_halo[0, m], halo[P3, 0, m], halo[SAT, 0, m]), at_x(m, 1))
        saturate_at(m, end, at_x(m, end - 1), (s_halo[1, m], halo[P3, 1, m], halo[SAT, 1, m]))
    acc = lax.fori_loop(0, nw, gather(sn_rows, nw), acc, unroll=8)
    found[0, 0] = acc

    def found_copy(k, m):
        return pltpu.make_async_remote_copy(
            src_ref=found.at[0, 0], dst_ref=found.at[m, k],
            send_sem=found_send.at[m, k], recv_sem=found_recv.at[m, k],
            device_id={"cell": lax.rem(cell + k, ncell), "member": mem if m == 0 else other},
            device_id_type=MESH,
        )

    def each_found(act_on):
        def step(k, carry):
            act_on(found_copy(k, 1))

            @pl.when(k > 0)
            def _():
                act_on(found_copy(k, 0))

            return carry

        lax.fori_loop(0, ncell, step, 0)

    each_found(lambda c: c.start())
    each_found(lambda c: c.wait_recv())

    own = found[0, 0]
    far = found[1, 0]
    for k in range(1, ncell):
        own = own + found[0, k]
        far = far + found[1, k]
    own_out[...] = own
    far_out[...] = far

    peer.wait_recv()
    peer.wait_send()
    each_found(lambda c: c.wait_send())
    for f, ref in ((LP, lp_hbm), (PR, pr_hbm), (SAT, sat_hbm), (Q1, qb), (Q2, qa), (P3, p3)):
        for g in range(HALVES):
            sent_edges(f, ref, g)

    @pl.when(has_left)
    def _():
        act_copy(1).wait_send()

    @pl.when(has_right)
    def _():
        act_copy(0).wait_send()


def update_kernel(
    lp, lp_peer, p3, snew, own_in, far_in, obs, var, noise,
    upd_out, pr_out, sat_out, pred_out,
    upd, wcol, out_sems,
):
    md, nx, cy, cz = lp.shape
    put_p = pltpu.make_async_copy(p3, pr_out, out_sems.at[0])
    put_s = pltpu.make_async_copy(snew, sat_out, out_sems.at[1])
    put_p.start()
    put_s.start()
    mem = lax.axis_index("member")
    own = own_in[...]
    far = far_in[...]
    pred_out[...] = own
    nd = own.shape[1]
    members = 2 * md
    root = float(members - 1) ** 0.5
    both = jnp.concatenate([own, far], axis=0)
    spread = (both - jnp.mean(both, axis=0, keepdims=True)) * (1.0 / root)
    dvar = INFLATION_FACTOR * var[...]
    first = pl.multiple_of(mem * md, md)
    misfit = obs[...] + jnp.sqrt(dvar) * noise[pl.ds(first, md), :] - own
    stack = jnp.concatenate([spread, misfit, jnp.zeros((nd - 3 * md, nd), jnp.float32)], axis=0)
    aug = lax.dot_general(
        spread / dvar, stack, (((1,), (1,)), ((), ())),
        precision=lax.Precision.HIGHEST, preferred_element_type=jnp.float32,
    )
    rid = lax.broadcasted_iota(jnp.int32, (members, nd), 0)
    cid = lax.broadcasted_iota(jnp.int32, (members, nd), 1)
    aug = aug + jnp.where(rid == cid, 1.0, 0.0)
    for k in range(members):
        line = aug[k : k + 1, :] / aug[k : k + 1, k : k + 1]
        aug = jnp.where(rid == k, line, aug - aug[:, k : k + 1] * line)
    for j in range(md):
        wcol[j] = jnp.broadcast_to(aug[:, members + j : members + j + 1] * (1.0 / root), (members, cz))

    parts = 4
    share = nx // parts

    def put_u(i):
        return pltpu.make_async_copy(
            upd.at[:, pl.ds(i * share, share)], upd_out.at[:, pl.ds(i * share, share)], out_sems.at[2 + i]
        )

    def mix(x, carry):
        fields = [lp[i, x] for i in range(md)] + [lp_peer[i, x] for i in range(md)]
        for j in range(md):
            total = fields[j]
            for i in range(members):
                total = total + wcol[j, i : i + 1, :] * fields[i]
            upd[j, x] = total
        return carry

    for i in range(parts):
        lax.fori_loop(i * share, (i + 1) * share, mix, 0)
        put_u(i).start()
    put_p.wait()
    put_s.wait()
    for i in range(parts):
        put_u(i).wait()


def local(
    log_perm, pressure, saturation, storage, source, active, wells, observed, observation_variance, noise,
):
    md, nx, cy, cz = log_perm.shape
    ncell = lax.axis_size("cell")
    nd = observed.shape[0]
    field = (md, nx, cy, cz)
    plane = (nx, cy, cz)
    f32 = jnp.float32
    any_spec = pl.BlockSpec(memory_space=pltpu.HBM)
    vmem_spec = pl.BlockSpec(memory_space=pltpu.VMEM)
    dma = pltpu.SemaphoreType.DMA
    limit = 24 * 1024 * 1024
    lp, lp_peer, p3, snew, own, far = pl.pallas_call(
        functools.partial(kernel, ncell),
        out_shape=[pltpu.VMEM(field, f32)] * 4 + [pltpu.VMEM((md, nd), f32)] * 2,
        in_specs=[any_spec] * 6 + [pl.BlockSpec(memory_space=pltpu.SMEM)],
        out_specs=[vmem_spec] * 6,
        scratch_shapes=[
            pltpu.VMEM(field, f32), pltpu.VMEM(field, f32),
            pltpu.VMEM(plane, f32), pltpu.VMEM(plane, f32), pltpu.VMEM(plane, jnp.int32),
            *[pltpu.VMEM(field, f32) for _ in range(5)],
            pltpu.VMEM((6, 2, md, cy, cz), f32),
            pltpu.VMEM((2, cy, cz), jnp.int32),
            pltpu.VMEM((2, md, cy, cz), f32),
            pltpu.VMEM((2, md, cy, cz), f32),
            pltpu.VMEM((2, ncell, md, nd), f32),
            dma((6,)), dma((6, 2, HALVES)), dma((6, 2, HALVES)), dma((2,)), dma((2,)),
            dma, dma, dma((2, ncell)), dma((2, ncell)),
        ],
        compiler_params=pltpu.CompilerParams(collective_id=0, has_side_effects=True, vmem_limit_bytes=limit),
    )(log_perm, pressure, saturation, storage, source, active, wells)
    return pl.pallas_call(
        update_kernel,
        out_shape=[jax.ShapeDtypeStruct(field, f32)] * 3 + [jax.ShapeDtypeStruct((md, nd), f32)],
        in_specs=[vmem_spec] * 9,
        out_specs=[pl.BlockSpec(memory_space=pltpu.HBM)] * 3 + [vmem_spec],
        scratch_shapes=[pltpu.VMEM(field, f32), pltpu.VMEM((md, 2 * md, cz), f32), dma((6,))],
        compiler_params=pltpu.CompilerParams(vmem_limit_bytes=limit),
    )(
        lp, lp_peer, p3, snew, own, far,
        observed.reshape(1, nd), observation_variance.reshape(1, nd), noise,
    )


def solution(mesh):
    block = P("member", ("group", "cell"), None, None)
    shared = P(("group", "cell"), None, None)
    in_specs = (block, block, block, shared, shared, shared, P("group"), P("group"), P("group"), P("group", None))
    out_specs = (block, block, block, P(("group", "member"), None))
    return jax.shard_map(local, mesh=mesh, in_specs=in_specs, out_specs=out_specs, check_vma=False)
```

```python
import functools
import jax
import jax.numpy as jnp
from jax import lax
from jax.experimental import pallas as pl
from jax.experimental.pallas import tpu as pltpu
from jax.sharding import PartitionSpec as P

ITERS = 3
INFLATION_FACTOR = 4.0
TIME_STEP = 0.02
MESH = pl.DeviceIdType.MESH
LP, PR, SAT, Q1, Q2, P3 = range(6)
HALVES = 2


def kernel(
    ncell,
    lp_hbm, pr_hbm, sat_hbm, sto_hbm, src_hbm, act_hbm, wells,
    lp, lp_peer, p3, snew, own_out, far_out,
    pr, sat, sto, src, act,
    s, qa, qb, rhs, rbal,
    halo, act_halo, s_halo, q0_halo, found,
    load_sems, send_sems, recv_sems, act_send, act_recv,
    peer_send, peer_recv, found_send, found_recv,
):
    md, nx, cy, cz = lp.shape
    cell = lax.axis_index("cell")
    mem = lax.axis_index("member")
    other = 1 - mem
    has_left = cell > 0
    has_right = cell < ncell - 1
    left = jnp.maximum(cell - 1, 0)
    right = jnp.minimum(cell + 1, ncell - 1)

    loads = [
        pltpu.make_async_copy(a, b, load_sems.at[i])
        for i, (a, b) in enumerate(
            [(act_hbm, act), (lp_hbm, lp), (pr_hbm, pr), (sto_hbm, sto), (src_hbm, src), (sat_hbm, sat)]
        )
    ]
    for c in loads:
        c.start()

    barrier = pltpu.get_barrier_semaphore()

    def greet(k, carry):
        to = lax.rem(cell + k, ncell)
        pl.semaphore_signal(barrier, inc=1, device_id={"cell": to, "member": other}, device_id_type=MESH)

        @pl.when(k > 0)
        def _():
            pl.semaphore_signal(barrier, inc=1, device_id={"cell": to, "member": mem}, device_id_type=MESH)

        return carry

    lax.fori_loop(0, ncell, greet, 0)
    pl.semaphore_wait(barrier, 2 * ncell - 1)

    def remote(source, dest, ssem, rsem, to):
        return pltpu.make_async_remote_copy(
            src_ref=source, dst_ref=dest, send_sem=ssem, recv_sem=rsem,
            device_id={"cell": to}, device_id_type=MESH,
        )

    half = md // HALVES
    groups = [pl.ds(g * half, half) for g in range(HALVES)]

    def edge_copy(f, side, ref, g):
        x = nx - 1 if side == 0 else 0
        to = right if side == 0 else left
        part = groups[g]
        return remote(
            ref.at[part, x], halo.at[f, side, part], send_sems.at[f, side, g], recv_sems.at[f, side, g], to
        )

    def act_copy(side):
        x = nx - 1 if side == 0 else 0
        to = right if side == 0 else left
        return remote(act_hbm.at[x], act_halo.at[side], act_send.at[side], act_recv.at[side], to)

    def send_edges(f, ref, g):
        @pl.when(has_left)
        def _():
            edge_copy(f, 1, ref, g).start()

        @pl.when(has_right)
        def _():
            edge_copy(f, 0, ref, g).start()

    def wait_edges(f, ref, g):
        @pl.when(has_left)
        def _():
            edge_copy(f, 0, ref, g).wait_recv()

        @pl.when(has_right)
        def _():
            edge_copy(f, 1, ref, g).wait_recv()

    def sent_edges(f, ref, g):
        @pl.when(has_left)
        def _():
            edge_copy(f, 1, ref, g).wait_send()

        @pl.when(has_right)
        def _():
            edge_copy(f, 0, ref, g).wait_send()

    @pl.when(has_left)
    def _():
        act_copy(1).start()

    @pl.when(has_right)
    def _():
        act_copy(0).start()

    for g in range(HALVES):
        send_edges(LP, lp_hbm, g)
        send_edges(PR, pr_hbm, g)
    for g in range(HALVES):
        send_edges(SAT, sat_hbm, g)
    peer = pltpu.make_async_remote_copy(
        src_ref=lp_hbm, dst_ref=lp_peer, send_sem=peer_send, recv_sem=peer_recv,
        device_id={"member": other}, device_id_type=MESH,
    )
    peer.start()

    @pl.when(jnp.logical_not(has_left))
    def _():
        for f in range(6):
            halo[f, 0] = jnp.zeros((md, cy, cz), jnp.float32)
        s_halo[0] = jnp.zeros((md, cy, cz), jnp.float32)

    @pl.when(jnp.logical_not(has_right))
    def _():
        for f in range(6):
            halo[f, 1] = jnp.zeros((md, cy, cz), jnp.float32)
        s_halo[1] = jnp.zeros((md, cy, cz), jnp.float32)

    lane = lax.broadcasted_iota(jnp.int32, (1, cy, cz), 2)
    row = lax.broadcasted_iota(jnp.int32, (1, cy, cz), 1)

    def z_up(v):
        return pltpu.roll(v, cz - 1, 2)

    def z_down(v):
        return pltpu.roll(v, 1, 2)

    def y_up(v):
        return pltpu.roll(v, cy - 1, 1)

    def y_down(v):
        return pltpu.roll(v, 1, 1)

    def plane_sum(q):
        return (
            jnp.where(lane == cz - 1, 0.0, z_up(q))
            + jnp.where(lane == 0, 0.0, z_down(q))
            + jnp.where(row == cy - 1, 0.0, y_up(q))
            + jnp.where(row == 0, 0.0, y_down(q))
        )

    loads[0].wait()
    loads[1].wait()
    for i in (2, 3, 4):
        loads[i].wait()

    def prepare(x, carry):
        sc = act[x].astype(jnp.float32)[None] * jnp.exp(0.5 * lp[:, x])
        s[:, x] = sc
        pc = pr[:, x]
        qa[:, x] = sc * pc
        rhs[:, x] = sto[x][None] * pc + src[x][None]
        return carry

    lax.fori_loop(0, nx, prepare, 0)

    def balance_at(m, x, below, above):
        sc = s[m, x]
        total = sto[x][None] + sc * (below + above + plane_sum(sc))
        rbal[m, x] = 1.0 / total

    def sweep_at(m, x, below, above, old, new, last):
        sc = s[m, x]
        p = (rhs[m, x] + sc * (below + above + plane_sum(old[m, x]))) * rbal[m, x]
        new[m, x] = p if last else sc * p

    inner = nx - 2
    width = max(d for d in range(1, 8) if inner % d == 0)

    def interior(f):
        def step(i, carry):
            for j in range(width):
                f(1 + i * width + j)
            return carry

        lax.fori_loop(0, inner // width, step, 0)

    end = nx - 1

    def first_inside(m):
        def f(x):
            balance_at(m, x, s[m, x - 1], s[m, x + 1])
            sweep_at(m, x, qa[m, x - 1], qa[m, x + 1], qa, qb, False)

        interior(f)

    for m in groups:
        first_inside(m)

    for g, m in enumerate(groups):
        for side, there in ((0, has_left), (1, has_right)):
            @pl.when(there)
            def _(side=side, g=g, m=m):
                if g == 0:
                    act_copy(side).wait_recv()
                edge_copy(LP, side, lp_hbm, g).wait_recv()
                edge_copy(PR, side, pr_hbm, g).wait_recv()
                s_halo[side, m] = act_halo[side].astype(jnp.float32)[None] * jnp.exp(0.5 * halo[LP, side, m])

            q0_halo[side, m] = s_halo[side, m] * halo[PR, side, m]
        balance_at(m, 0, s_halo[0, m], s[m, 1])
        sweep_at(m, 0, q0_halo[0, m], qa[m, 1], qa, qb, False)
        balance_at(m, end, s[m, end - 1], s_halo[1, m])
        sweep_at(m, end, qa[m, end - 1], q0_halo[1, m], qa, qb, False)
        send_edges(Q1, qb, g)

    for f, old, new, nf, last in ((Q1, qb, qa, Q2, False), (Q2, qa, p3, P3, True)):
        for g, m in enumerate(groups):
            interior(lambda x: sweep_at(m, x, old[m, x - 1], old[m, x + 1], old, new, last))
            wait_edges(f, old, g)
            sweep_at(m, 0, halo[f, 0, m], old[m, 1], old, new, last)
            sweep_at(m, end, old[m, end - 1], halo[f, 1, m], old, new, last)
            send_edges(nf, new, g)
    loads[5].wait()

    def face(sn, pn, tn, pc, tc):
        d = pn - pc
        return sn * (d * jnp.where(d > 0, tn, tc))

    def saturate_at(m, x, below, above):
        sc = s[m, x]
        pc = p3[m, x]
        raw = sat[m, x]
        tc = raw * raw
        bs, bp, bt = below
        as_, ap, at = above
        change = face(bs, bp, bt * bt, pc, tc) + face(as_, ap, at * at, pc, tc)
        gz = sc * face(jnp.where(lane == cz - 1, 0.0, z_up(sc)), z_up(pc), z_up(tc), pc, tc)
        gy = sc * face(jnp.where(row == cy - 1, 0.0, y_up(sc)), y_up(pc), y_up(tc), pc, tc)
        change = sc * change + (gz - z_down(gz)) + (gy - y_down(gy))
        snew[m, x] = raw + change * (TIME_STEP / sto[x])[None]

    def at_x(m, x):
        return s[m, x], p3[m, x], sat[m, x]

    for m in groups:
        interior(lambda x: saturate_at(m, x, at_x(m, x - 1), at_x(m, x + 1)))

    nw = wells.shape[0]
    cells_dev = nx * cy * cz
    col = lax.broadcasted_iota(jnp.int32, (md, 2 * nw), 1)
    p3_rows = p3.reshape(md * nx * cy, cz)
    sn_rows = snew.reshape(md * nx * cy, cz)

    def gather(rows, first):
        def one(w, acc):
            at = wells[w] - cell * cells_dev
            inside = jnp.logical_and(at >= 0, at < cells_dev)
            at = jnp.clip(at, 0, cells_dev - 1)
            line = at // cz
            z = at - line * cz
            v = rows[pl.ds(line, md, stride=nx * cy), :]
            v = pltpu.roll(v, lax.rem(first + w - z + cz, cz), 1)
            keep = jnp.where(inside, w + first, -1)
            return jnp.where(col == keep, v, acc)

        return one

    acc = lax.fori_loop(0, nw, gather(p3_rows, 0), jnp.zeros((md, 2 * nw), jnp.float32), unroll=8)

    for g, m in enumerate(groups):
        wait_edges(SAT, sat_hbm, g)
        wait_edges(P3, p3, g)
        saturate_at(m, 0, (s_halo[0, m], halo[P3, 0, m], halo[SAT, 0, m]), at_x(m, 1))
        saturate_at(m, end, at_x(m, end - 1), (s_halo[1, m], halo[P3, 1, m], halo[SAT, 1, m]))
    acc = lax.fori_loop(0, nw, gather(sn_rows, nw), acc, unroll=8)
    found[0, 0] = acc

    def found_copy(k, m):
        return pltpu.make_async_remote_copy(
            src_ref=found.at[0, 0], dst_ref=found.at[m, k],
            send_sem=found_send.at[m, k], recv_sem=found_recv.at[m, k],
            device_id={"cell": lax.rem(cell + k, ncell), "member": mem if m == 0 else other},
            device_id_type=MESH,
        )

    def each_found(act_on):
        def step(k, carry):
            act_on(found_copy(k, 1))

            @pl.when(k > 0)
            def _():
                act_on(found_copy(k, 0))

            return carry

        lax.fori_loop(0, ncell, step, 0)

    each_found(lambda c: c.start())
    each_found(lambda c: c.wait_recv())

    own = found[0, 0]
    far = found[1, 0]
    for k in range(1, ncell):
        own = own + found[0, k]
        far = far + found[1, k]
    own_out[...] = own
    far_out[...] = far

    peer.wait_recv()
    peer.wait_send()
    each_found(lambda c: c.wait_send())
    for f, ref in ((LP, lp_hbm), (PR, pr_hbm), (SAT, sat_hbm), (Q1, qb), (Q2, qa), (P3, p3)):
        for g in range(HALVES):
            sent_edges(f, ref, g)

    @pl.when(has_left)
    def _():
        act_copy(1).wait_send()

    @pl.when(has_right)
    def _():
        act_copy(0).wait_send()


def update_kernel(
    lp, lp_peer, p3, snew, own_in, far_in, obs, var, noise,
    upd_out, pr_out, sat_out, pred_out,
    upd, wcol, obs_v, var_v, noise_v, out_sems, in_sems,
):
    md, nx, cy, cz = lp.shape
    gets = [
        pltpu.make_async_copy(a, b, in_sems.at[i])
        for i, (a, b) in enumerate([(obs, obs_v), (var, var_v), (noise, noise_v)])
    ]
    for c in gets:
        c.start()
    put_p = pltpu.make_async_copy(p3, pr_out, out_sems.at[0])
    put_s = pltpu.make_async_copy(snew, sat_out, out_sems.at[1])
    put_p.start()
    put_s.start()
    mem = lax.axis_index("member")
    own = own_in[...]
    far = far_in[...]
    pred_out[...] = own
    nd = own.shape[1]
    members = 2 * md
    root = float(members - 1) ** 0.5
    both = jnp.concatenate([own, far], axis=0)
    spread = (both - jnp.mean(both, axis=0, keepdims=True)) * (1.0 / root)
    for c in gets:
        c.wait()
    dvar = INFLATION_FACTOR * var_v[...]
    first = pl.multiple_of(mem * md, md)
    misfit = obs_v[...] + jnp.sqrt(dvar) * noise_v[pl.ds(first, md), :] - own
    stack = jnp.concatenate([spread, misfit, jnp.zeros((nd - 3 * md, nd), jnp.float32)], axis=0)
    aug = lax.dot_general(
        spread / dvar, stack, (((1,), (1,)), ((), ())),
        precision=lax.Precision.HIGHEST, preferred_element_type=jnp.float32,
    )
    rid = lax.broadcasted_iota(jnp.int32, (members, nd), 0)
    cid = lax.broadcasted_iota(jnp.int32, (members, nd), 1)
    aug = aug + jnp.where(rid == cid, 1.0, 0.0)
    for k in range(members):
        line = aug[k : k + 1, :] / aug[k : k + 1, k : k + 1]
        aug = jnp.where(rid == k, line, aug - aug[:, k : k + 1] * line)
    for j in range(md):
        wcol[j] = jnp.broadcast_to(aug[:, members + j : members + j + 1] * (1.0 / root), (members, cz))

    parts = 4
    share = nx // parts

    def put_u(i):
        return pltpu.make_async_copy(
            upd.at[:, pl.ds(i * share, share)], upd_out.at[:, pl.ds(i * share, share)], out_sems.at[2 + i]
        )

    def mix(x, carry):
        fields = [lp[i, x] for i in range(md)] + [lp_peer[i, x] for i in range(md)]
        for j in range(md):
            total = fields[j]
            for i in range(members):
                total = total + wcol[j, i : i + 1, :] * fields[i]
            upd[j, x] = total
        return carry

    for i in range(parts):
        lax.fori_loop(i * share, (i + 1) * share, mix, 0)
        put_u(i).start()
    put_p.wait()
    put_s.wait()
    for i in range(parts):
        put_u(i).wait()


def local(
    log_perm, pressure, saturation, storage, source, active, wells, observed, observation_variance, noise,
):
    md, nx, cy, cz = log_perm.shape
    ncell = lax.axis_size("cell")
    nd = observed.shape[0]
    field = (md, nx, cy, cz)
    plane = (nx, cy, cz)
    f32 = jnp.float32
    any_spec = pl.BlockSpec(memory_space=pltpu.HBM)
    vmem_spec = pl.BlockSpec(memory_space=pltpu.VMEM)
    dma = pltpu.SemaphoreType.DMA
    lp, lp_peer, p3, snew, own, far = pl.pallas_call(
        functools.partial(kernel, ncell),
        out_shape=[pltpu.VMEM(field, f32)] * 4 + [pltpu.VMEM((md, nd), f32)] * 2,
        in_specs=[any_spec] * 6 + [pl.BlockSpec(memory_space=pltpu.SMEM)],
        out_specs=[vmem_spec] * 6,
        scratch_shapes=[
            pltpu.VMEM(field, f32), pltpu.VMEM(field, f32),
            pltpu.VMEM(plane, f32), pltpu.VMEM(plane, f32), pltpu.VMEM(plane, jnp.int32),
            *[pltpu.VMEM(field, f32) for _ in range(5)],
            pltpu.VMEM((6, 2, md, cy, cz), f32),
            pltpu.VMEM((2, cy, cz), jnp.int32),
            pltpu.VMEM((2, md, cy, cz), f32),
            pltpu.VMEM((2, md, cy, cz), f32),
            pltpu.VMEM((2, ncell, md, nd), f32),
            dma((6,)), dma((6, 2, HALVES)), dma((6, 2, HALVES)), dma((2,)), dma((2,)),
            dma, dma, dma((2, ncell)), dma((2, ncell)),
        ],
        compiler_params=pltpu.CompilerParams(collective_id=0, has_side_effects=True, vmem_limit_bytes=58 * 1024 * 1024),
    )(log_perm, pressure, saturation, storage, source, active, wells)
    return pl.pallas_call(
        update_kernel,
        out_shape=[jax.ShapeDtypeStruct(field, f32)] * 3 + [jax.ShapeDtypeStruct((md, nd), f32)],
        in_specs=[vmem_spec] * 6 + [any_spec] * 3,
        out_specs=[pl.BlockSpec(memory_space=pltpu.HBM)] * 3 + [vmem_spec],
        scratch_shapes=[
            pltpu.VMEM(field, f32), pltpu.VMEM((md, 2 * md, cz), f32),
            pltpu.VMEM((1, nd), f32), pltpu.VMEM((1, nd), f32), pltpu.VMEM((2 * md, nd), f32), dma((6,)), dma((3,)),
        ],
        compiler_params=pltpu.CompilerParams(vmem_limit_bytes=24 * 1024 * 1024),
    )(
        lp, lp_peer, p3, snew, own, far,
        observed.reshape(1, nd), observation_variance.reshape(1, nd), noise,
    )


def solution(mesh):
    block = P("member", ("group", "cell"), None, None)
    shared = P(("group", "cell"), None, None)
    in_specs = (block, block, block, shared, shared, shared, P("group"), P("group"), P("group"), P("group", None))
    out_specs = (block, block, block, P(("group", "member"), None))
    return jax.shard_map(local, mesh=mesh, in_specs=in_specs, out_specs=out_specs, check_vma=False)
```
